256 devices in a mesh: gx: 4 (over x_lo, core), gy: 8 (over y, x_hi), gz: 8 (over z).
Axes of the slice: x: 4 (x_hi: 2, x_lo: 2; x = x_hi * 2 + x_lo), y: 4, z: 8, core: 2. Of those that a mesh axis runs over, the one named last changes fastest.
Arguments:
- atoms: float32 [4, 4, 8, 512, 128], P(None, 'gx', 'gy', 'gz'), as said below
- velocities: float32 [3, 4, 8, 512, 128], P(None, 'gx', 'gy', 'gz'), may hold values from -4 to 4
- inverse_mass: float32 [4, 8, 512, 128], P('gx', 'gy', 'gz'), as said below
- bond_partner: int32 [4, 8, 512, 128], P('gx', 'gy', 'gz'), may hold values from 0 to 127, as said below
- cluster_pairs: int32 [2, 4, 8, 2048], P(None, 'gx', 'gy', 'gz'), may hold values from 0 to 575, as said below
- pair_count: int32 [4, 8, 8], P('gx', 'gy', 'gz'), may hold values from 64 to 256, as said below
Outputs:
- forces: float32 [3, 4, 8, 512, 128], P(None, 'gx', 'gy', 'gz')
- new_velocities: float32 [3, 4, 8, 512, 128], P(None, 'gx', 'gy', 'gz')
The draws below stay inside these ranges and needn't reach their ends.
Inputs may be any that keep to these rules, and one draw needn't show every extreme that they name: `cluster_pairs`: row 0 names a tower slot below 192, row 1 a plate slot, in the slot numbering of the steps. Only the first pair_count slots of a device are live; the others hold arbitrary valid slots. No pair names the device's own cluster c twice (tower slot 64 + c with plate slot 256 + c). `pair_count`: some device has exactly 256 live pairs and some device exactly 64. `bond_partner`: A hydrogen names the heavy atom of its update group; every other atom names itself; no atom names a hydrogen. Update groups lie within aligned runs of four atoms of a cluster, whose first atom is heavy. `atoms`: A hydrogen lies 0.08 to 0.18 nm from the heavy atom it names. `inverse_mass`: 1 / 1.008 for hydrogens, 1 / 32 to 1 / 12 for other atoms.
All inputs are finite; a program needn't handle non-finite values.
Results may differ from the reference program's by a relative error of at most 0.0003.
Values sent between devices are 32-bit elements; how exact they have to be, the bound alone decides.
No kernel may reach another device: no remote copies, remote signals or barrier semaphores. Data moves between devices by JAX's collectives and lax.ppermute only.
A program may use at most 64 MiB of HBM per device.

```python
import math
import jax
import jax.numpy as jnp
from jax import lax

ATOMS = 128
CL = 64
PMAX = 256
ITERS = 2
CLUS = 512
N_GX = 4
N_GY = 8
N_GZ = 8


def lattice_side():
    side = 1
    while side * side * side < CL:
        side = side + 1
    return side


def lattice_cells():
    side = lattice_side()
    cells = jnp.arange(CL, dtype=jnp.int32)
    return (cells % side, cells // side % side, cells // (side * side))


def group_layout(key):
    quads = jax.random.randint(jax.random.fold_in(key, 101), (N_GX, N_GY, CLUS, ATOMS // 4), 0, 4)
    corner = jnp.arange(4, dtype=jnp.int32)
    hydro = (corner >= 1) & (corner <= quads[..., None])
    heads = (jnp.arange(ATOMS // 4, dtype=jnp.int32) * 4)[:, None]
    partner = jnp.where(hydro, heads + 0 * corner, heads + corner)
    shape = (N_GX, N_GY, CLUS, ATOMS)
    return (partner.reshape(shape).astype(jnp.int32), hydro.reshape(shape))


def draw_bond_partner(key, part):
    partner, hydro = group_layout(key)
    return partner


def draw_atoms(key, part):
    partner, hydro = group_layout(key)
    key = jax.random.fold_in(key, 2)
    keys = jax.random.split(key, 4)
    side = lattice_side()
    edge = 2.4 * (CL / 8.0) ** (1.0 / 3.0)
    spacing = edge / side
    shape = (3, N_GX, N_GY, CLUS, ATOMS)
    cell_x, cell_y, cell_z = lattice_cells()
    root = jnp.stack([cell_x, cell_y, cell_z]).astype(jnp.float32)
    root = jnp.tile(root, (1, N_GZ))[:, None, None, :, None]
    inside = jax.random.uniform(keys[0], shape, jnp.float32, 0.0, 1.0)
    heavy = (root + inside) * spacing
    reach = jax.random.uniform(keys[1], shape, jnp.float32, 0.05, 0.1)
    signs = jax.random.randint(keys[2], shape, 0, 2).astype(jnp.float32) * 2.0 - 1.0
    anchor = jnp.take_along_axis(heavy, jnp.broadcast_to(partner, shape), axis=-1)
    coords = jnp.where(hydro[None], anchor + signs * reach, heavy)
    charge = jnp.clip(0.4 * jax.random.normal(keys[3], shape[1:], jnp.float32), -1.5, 1.5)
    return jnp.concatenate([coords, charge[None]], axis=0).astype(jnp.float32)


def draw_inverse_mass(key, part):
    partner, hydro = group_layout(key)
    key = jax.random.fold_in(key, 3)
    shape = (N_GX, N_GY, CLUS, ATOMS)
    heavy = jnp.exp(jax.random.uniform(key, shape, jnp.float32, math.log(1.0 / 32.0), math.log(1.0 / 12.0)))
    return jnp.where(hydro, 1.0 / 1.008, heavy).astype(jnp.float32)


def draw_cluster_pairs(key, part):
    key = jax.random.fold_in(key, 4)
    keys = jax.random.split(key, 3)
    side = lattice_side()
    cell_x, cell_y, cell_z = lattice_cells()
    tower_slot = jnp.arange(3 * CL, dtype=jnp.int32)
    tower_member = tower_slot % CL
    tower_x = cell_x[tower_member]
    tower_y = cell_y[tower_member]
    tower_z = cell_z[tower_member] + (tower_slot // CL - 1) * side
    plate_slot = jnp.arange(9 * CL, dtype=jnp.int32)
    plate_member = plate_slot % CL
    plate_block = plate_slot // CL
    plate_x = cell_x[plate_member] + (plate_block // 3 - 1) * side
    plate_y = cell_y[plate_member] + (plate_block % 3 - 1) * side
    plate_z = cell_z[plate_member]
    close = (jnp.abs(tower_x[:, None] - plate_x[None, :]) <= 1) & (jnp.abs(tower_y[:, None] - plate_y[None, :]) <= 1) & (jnp.abs(tower_z[:, None] - plate_z[None, :]) <= 1)
    home = (tower_slot[:, None] >= CL) & (tower_slot[:, None] < 2 * CL) & (plate_slot[None, :] == tower_slot[:, None] + 3 * CL)
    size = 27 * CL * CL
    number = jnp.arange(size, dtype=jnp.int32)
    close_flat = close.reshape(-1).astype(jnp.int32)
    home_flat = home.reshape(-1)
    devices = N_GX * N_GY * N_GZ

    def one_device(index):
        noise = jax.random.randint(jax.random.fold_in(keys[0], index), (size,), 0, 8192)
        score = close_flat * 2 ** 30 + noise * 2 ** 17 + number
        score = jnp.where(home_flat, -1, score)
        best = lax.top_k(score, PMAX)[1].astype(jnp.int32)
        return jnp.stack([best // (9 * CL), best % (9 * CL)])
    chosen = lax.map(one_device, jnp.arange(devices, dtype=jnp.int32))
    tower = chosen[:, 0].reshape(-1)
    plate = chosen[:, 1].reshape(-1)
    spots = jax.random.randint(keys[2], (2,), 0, devices * PMAX)
    tower = tower.at[spots[0]].set(3 * CL - 1).reshape(N_GX, N_GY, N_GZ * PMAX)
    plate = plate.at[spots[1]].set(9 * CL - 1).reshape(N_GX, N_GY, N_GZ * PMAX)
    return jnp.stack([tower, plate]).astype(jnp.int32)


def draw_pair_count(key, part):
    key = jax.random.fold_in(key, 5)
    keys = jax.random.split(key, 5)
    shape = (N_GX, N_GY, N_GZ)
    layer = jax.random.randint(keys[0], (), 0, N_GZ)
    depth = lax.broadcasted_iota(jnp.int32, shape, 2)
    sparse = jax.random.randint(keys[1], shape, PMAX // 4, PMAX // 2 + 1)
    dense = jax.random.randint(keys[2], shape, 3 * PMAX // 4, PMAX + 1)
    counts = jnp.where(depth == layer, dense, sparse).reshape(-1)
    total = N_GX * N_GY * N_GZ
    first = jax.random.randint(keys[3], (), 0, total)
    second = (first + 1 + jax.random.randint(keys[4], (), 0, total - 1)) % total
    counts = counts.at[first].set(PMAX).at[second].set(PMAX // 4)
    return counts.reshape(shape).astype(jnp.int32)


def shard_levels(stream_key, extent, cuts, low, largest):
    factor_of = 1.0
    for dim, blocks in cuts:
        heights = jax.random.uniform(jax.random.fold_in(jax.random.fold_in(stream_key, 6), dim), (blocks,), jnp.float32, low / len(cuts), largest / len(cuts))
        factor_of = factor_of * jnp.repeat(jnp.exp(heights), extent[dim] // blocks).reshape((-1,) + (1,) * (len(extent) - 1 - dim))
    return factor_of


def bell_draw(rng, shape, deviation, most, cuts=(), kind=jnp.bfloat16):
    loudness = shard_levels(rng, shape, cuts, -0.22, 0.18) if cuts else 1.0
    values = jax.random.normal(rng, shape, jnp.float32) * deviation * loudness
    return jnp.minimum(jnp.maximum(values, -most), most).astype(kind)


def setup_inputs(seed: int = 0) -> dict:
    arg_keys = jax.random.split(jax.random.key(seed), 7)
    return {
        "atoms": draw_atoms(jax.random.fold_in(arg_keys[6], 71), 0),
        "velocities": bell_draw(arg_keys[1], (3, N_GX, N_GY, CLUS, ATOMS), 1.0, 4.0, ((1, 4), (2, 8), (3, 8)), jnp.float32),
        "inverse_mass": draw_inverse_mass(jax.random.fold_in(arg_keys[6], 71), 0),
        "bond_partner": draw_bond_partner(jax.random.fold_in(arg_keys[6], 71), 0),
        "cluster_pairs": draw_cluster_pairs(jax.random.fold_in(arg_keys[6], 71), 0),
        "pair_count": draw_pair_count(jax.random.fold_in(arg_keys[6], 71), 0),
    }


TIME_STEP = 0.002
FORCE_UNIT = 500.0
CUTOFF = 1.2
SOFT_CORE = 0.04

def edge_of(clusters):
    return 2.4 * (clusters / 8.0) ** (1.0 / 3.0)

def pair_kernel(tower_part, plate_part):
    apart = tower_part[:3, :, :, None] - plate_part[:3, :, None, :]
    spread = apart[0] * apart[0] + apart[1] * apart[1] + apart[2] * apart[2]
    weight = 1.0 / (spread + SOFT_CORE)
    taper = jnp.maximum(1.0 - spread * (1.0 / CUTOFF ** 2), 0.0)
    taper = taper * taper
    charges = tower_part[3, :, :, None] * plate_part[3, :, None, :]
    scalar = taper * charges * (weight * jnp.sqrt(weight) - 1.0 / CUTOFF ** 3)
    pulls = scalar[None] * apart
    return (lax.optimization_barrier(jnp.sum(pulls, axis=3)), -lax.optimization_barrier(jnp.sum(pulls, axis=2)))

def sweep_pairs(tower, plate, tower_index, plate_index, count, blocks):
    per_block = 32
    width = tower.shape[2]

    def visit(number, totals):
        tower_total, plate_total = totals
        first = number * per_block
        tower_rows = lax.dynamic_slice_in_dim(tower_index, first, per_block)
        plate_rows = lax.dynamic_slice_in_dim(plate_index, first, per_block)
        active = (first + jnp.arange(per_block, dtype=jnp.int32) < count).astype(tower.dtype)[None, :, None]
        tower_pull, plate_pull = pair_kernel(tower[:, tower_rows], plate[:, plate_rows])
        return (tower_total.at[:, tower_rows].add(tower_pull * active), plate_total.at[:, plate_rows].add(plate_pull * active))
    start = (jnp.zeros((3, tower.shape[1], width), tower.dtype), jnp.zeros((3, plate.shape[1], width), plate.dtype))
    return lax.fori_loop(0, blocks, visit, start)

def scatter_rows(delta, partner):
    flat = delta.reshape(3, -1, delta.shape[-1])
    links = partner.reshape(-1, partner.shape[-1])

    def one_row(values, targets):
        return jnp.zeros(values.shape, values.dtype).at[targets].add(values)
    summed = jax.vmap(jax.vmap(one_row), in_axes=(0, None))(flat, links)
    return summed.reshape(delta.shape)

def hold_bonds(coords, kicked, inverse_mass, partner):
    place = jnp.arange(partner.shape[-1], dtype=jnp.int32)
    hydro = partner != place
    spread_index = jnp.broadcast_to(partner, coords.shape)
    bond = coords - jnp.take_along_axis(coords, spread_index, axis=-1)
    bond_square = lax.optimization_barrier(jnp.sum(bond * bond, axis=0))
    paired = inverse_mass + jnp.take_along_axis(inverse_mass, partner, axis=-1)
    shift = TIME_STEP * kicked
    for sweep in range(ITERS):
        gap = bond + (shift - jnp.take_along_axis(shift, spread_index, axis=-1))
        excess = lax.optimization_barrier(jnp.sum(gap * gap, axis=0)) - bond_square
        slope = 2.0 * lax.optimization_barrier(jnp.sum(gap * bond, axis=0)) * paired
        factor = jnp.where(hydro, excess / jnp.where(hydro, slope, 1.0), 0.0)
        delta = factor[None] * bond
        back = scatter_rows(delta, partner)
        shift = shift + inverse_mass[None] * (back - delta)
    return shift / TIME_STEP

def reference(atoms, velocities, inverse_mass, bond_partner, cluster_pairs, pair_count):
    edge = edge_of(CL)
    total = N_GX * N_GY * N_GZ
    grid = atoms.reshape(4, N_GX, N_GY, N_GZ, CL, ATOMS)
    towers = []
    for depth in (-1, 0, 1):
        lifted = jnp.array([0.0, 0.0, depth * edge, 0.0], jnp.float32).reshape(4, 1, 1, 1, 1, 1)
        towers.append(jnp.roll(grid, -depth, axis=3) + lifted)
    tower = jnp.stack(towers, axis=4).reshape(4, total, 3 * CL, ATOMS)
    plates = []
    for across in (-1, 0, 1):
        for along in (-1, 0, 1):
            lifted = jnp.array([across * edge, along * edge, 0.0, 0.0], jnp.float32).reshape(4, 1, 1, 1, 1, 1)
            plates.append(jnp.roll(grid, (-across, -along), axis=(1, 2)) + lifted)
    plate = jnp.stack(plates, axis=4).reshape(4, total, 9 * CL, ATOMS)
    listing = cluster_pairs.reshape(2, total, PMAX)
    counts = pair_count.reshape(total)

    def device_forces(packed):
        tower_zone, plate_zone, tower_index, plate_index, count = packed
        return sweep_pairs(tower_zone, plate_zone, tower_index, plate_index, count, PMAX // 32)
    tower_force, plate_force = lax.map(device_forces, (jnp.moveaxis(tower, 1, 0), jnp.moveaxis(plate, 1, 0), listing[0], listing[1], counts))
    tower_force = tower_force.reshape(N_GX, N_GY, N_GZ, 3, 3, CL, ATOMS)
    plate_force = plate_force.reshape(N_GX, N_GY, N_GZ, 3, 3, 3, CL, ATOMS)
    owned = jnp.zeros((N_GX, N_GY, N_GZ, 3, CL, ATOMS), jnp.float32)
    for slot, depth in enumerate((-1, 0, 1)):
        owned = owned + jnp.roll(tower_force[:, :, :, :, slot], depth, axis=2)
    for first_slot, across in enumerate((-1, 0, 1)):
        for second_slot, along in enumerate((-1, 0, 1)):
            owned = owned + jnp.roll(plate_force[:, :, :, :, first_slot, second_slot], (across, along), axis=(0, 1))
    forces = jnp.moveaxis(owned, 3, 0).reshape(3, N_GX, N_GY, CL * N_GZ, ATOMS)
    kicked = velocities + TIME_STEP * FORCE_UNIT * inverse_mass[None] * forces
    moved = hold_bonds(atoms[:3], kicked, inverse_mass, bond_partner)
    return (forces, moved)
```

```python
import functools

import jax
import jax.numpy as jnp
from jax import lax
from jax.experimental import pallas as pl
from jax.experimental.pallas import tpu as pltpu
from jax.sharding import PartitionSpec as P

ITERS = 2
TIME_STEP = 0.002
FORCE_UNIT = 500.0
CUTOFF = 1.2
SOFT_CORE = 0.04
SCALE = 1.0 / CUTOFF
CORE = SOFT_CORE / CUTOFF**2
STRENGTH = 1.0 / CUTOFF**2
HIGH, LOW = 8, 16
BLOCK = 2
SLOTS = 272
FIRST_OWN = 48
f32 = jnp.float32


def passed_along(value, axis, steps):
    count = lax.axis_size(axis)
    pairs = [(source, (source + steps) % count) for source in range(count)]
    return lax.ppermute(value, axis, pairs)


def plus(total, term):
    return term if total is None else total + term


def turned(value, shift):
    return value if shift % 128 == 0 else pltpu.roll(value, shift % 128, 1)


def eight_pairs(tower, plate, spun, pulled):
    tower_planes = [tower[8 * c : 8 * c + 8, :] for c in range(4)]
    plate_planes = [plate[8 * c : 8 * c + 8, :] for c in range(4)]
    tower_force = [None] * 3
    plate_force = [None] * 3
    rounds = HIGH // BLOCK
    for turn in range(rounds):
        coarse = [turn * BLOCK + u for u in range(BLOCK)]
        ahead = [[turned(v, -LOW * h) for v in tower_planes] for h in coarse]
        held = [[None] * 3 for _ in coarse]
        for low in range(LOW):
            if turn == 0:
                beside = [turned(v, low) for v in plate_planes]
                for c in range(4):
                    spun[low * 4 + c] = beside[c]
            else:
                beside = [spun[low * 4 + c] for c in range(4)]
            totals = [None if turn == 0 else pulled[low * 3 + c] for c in range(3)]
            for u in range(BLOCK):
                apart = [ahead[u][c] - beside[c] for c in range(3)]
                spread = apart[0] * apart[0] + apart[1] * apart[1] + apart[2] * apart[2]
                root = lax.rsqrt(spread + CORE)
                taper = jnp.maximum(1.0 - spread, 0.0)
                charges = ahead[u][3] * beside[3]
                scalar = (taper * taper) * charges * (root * root * root - 1.0)
                for c in range(3):
                    pull = scalar * apart[c]
                    held[u][c] = plus(held[u][c], pull)
                    totals[c] = plus(totals[c], pull)
            for c in range(3):
                if turn == rounds - 1:
                    plate_force[c] = plus(plate_force[c], turned(totals[c], -low))
                else:
                    pulled[low * 3 + c] = totals[c]
        for u, h in enumerate(coarse):
            for c in range(3):
                tower_force[c] = plus(tower_force[c], turned(held[u][c], LOW * h))
    return tower_force, plate_force


def sweep(listing, base, first, last, towers, plates, tower_total, plate_total, scratch):
    tower, plate, spun, pulled, tower_out, plate_out = scratch
    row = lax.broadcasted_iota(jnp.int32, (4, 128), 0)

    def step(group, _):
        places = []
        for u in range(8):
            number = first + group * 8 + u
            entry = listing[base + jnp.minimum(number, last - 1)]
            t, p = entry >> 10, entry & 1023
            tz, tc, pz, pc = t >> 6, t & 63, p >> 6, p & 63
            live = jnp.where(number < last, 1.0, 0.0)
            tower[pl.ds(u, 4, stride=8), :] = towers[
                pl.ds(tz * 256 + tc, 4, stride=64), :
            ] * jnp.where(row == 3, live, 1.0)
            plate[pl.ds(u, 4, stride=8), :] = plates[pl.ds(pz * 256 + pc, 4, stride=64), :]
            places.append((tz * 192 + tc, pz * 192 + pc))
        tower_force, plate_force = eight_pairs(tower, plate, spun, pulled)
        for c in range(3):
            tower_out[8 * c : 8 * c + 8, :] = tower_force[c]
            plate_out[8 * c : 8 * c + 8, :] = plate_force[c]
        for u, (t, p) in enumerate(places):
            tower_total[pl.ds(t, 3, stride=64), :] += tower_out[pl.ds(u, 3, stride=8), :]
            plate_total[pl.ds(p, 3, stride=64), :] -= plate_out[pl.ds(u, 3, stride=8), :]
        return 0

    groups = (jnp.maximum(last - first, 0) + 7) // 8
    lax.fori_loop(0, groups, step, 0)


def sweep_scratch():
    return [
        pltpu.VMEM((32, 128), f32),
        pltpu.VMEM((32, 128), f32),
        pltpu.VMEM((4 * LOW, 8, 128), f32),
        pltpu.VMEM((3 * LOW, 8, 128), f32),
        pltpu.VMEM((24, 128), f32),
        pltpu.VMEM((24, 128), f32),
    ]


def fill(target, block, source, lifts, strength):
    for c in range(4):
        start = block * 256 + c * 64
        values = source[c * 64 : c * 64 + 64, :]
        if c < 3:
            values = (values + lifts[c]) * SCALE if lifts[c] else values * SCALE
        elif strength:
            values = values * STRENGTH
        target[start : start + 64, :] = values


def edge_of(clusters):
    return 2.4 * (clusters / 8.0) ** (1.0 / 3.0)


def first_kernel(pairs, count, atoms, listing, own, towers, plates, totals, *scratch):
    fill(towers, 0, atoms, (0, 0, 0), True)
    fill(plates, 0, atoms, (0, 0, 0), False)
    own[...] = jnp.zeros_like(own)
    totals[...] = jnp.zeros_like(totals)
    live = count[0]

    def sort(number, counts):
        own_count, flat_count, across_count = counts
        t, p = pairs[0, number], pairs[1, number]
        block = p >> 6
        across = jnp.logical_or(block < 3, block >= 6)
        home = jnp.logical_and(block == 4, (t >> 6) == 1)
        own_place = own_count
        flat_place = SLOTS + flat_count
        across_place = 2 * SLOTS + across_count
        place = jnp.where(home, own_place, jnp.where(across, across_place, flat_place))
        plate_slot = jnp.where(across, jnp.where(block >= 6, p - 192, p), p - 192)
        entry = jnp.where(home, ((t & 63) << 10) | (p & 63), (t << 10) | plate_slot)
        listing[place] = entry
        one = jnp.int32(1)
        zero = jnp.int32(0)
        return (
            own_count + jnp.where(home, one, zero),
            flat_count + jnp.where(jnp.logical_or(home, across), zero, one),
            across_count + jnp.where(across, one, zero),
        )

    start = (jnp.int32(0), jnp.int32(0), jnp.int32(0))
    own_count, flat_count, across_count = lax.fori_loop(0, live, sort, start)
    listing[3 * SLOTS] = own_count
    listing[3 * SLOTS + 1] = flat_count
    listing[3 * SLOTS + 2] = across_count
    last = jnp.minimum(own_count, FIRST_OWN)
    sweep(listing, 0, 0, last, towers, plates, own, totals, scratch)
    own[...] += totals[...]


def second_kernel(
    listing, atoms, back, ahead, below, above, before,
    own, to_back, to_ahead, to_below, to_above,
    towers, plates, tower_total, plate_total, *scratch,
):
    edge = edge_of(atoms.shape[0] // 4)
    fill(towers, 0, below, (0, 0, -edge), True)
    fill(towers, 1, atoms, (0, 0, 0), True)
    fill(towers, 2, above, (0, 0, edge), True)
    fill(plates, 0, back, (0, -edge, 0), False)
    fill(plates, 1, atoms, (0, 0, 0), False)
    fill(plates, 2, ahead, (0, edge, 0), False)
    tower_total[...] = jnp.zeros_like(tower_total)
    plate_total[...] = jnp.zeros_like(plate_total)
    flat_count = listing[3 * SLOTS + 1]
    sweep(listing, SLOTS, 0, flat_count, towers, plates, tower_total, plate_total, scratch)
    own[...] = before[...] + tower_total[192:384, :] + plate_total[192:384, :]
    to_below[...] = tower_total[0:192, :]
    to_above[...] = tower_total[384:576, :]
    to_back[...] = plate_total[0:192, :]
    to_ahead[...] = plate_total[384:576, :]


def third_kernel(
    listing, atoms, below, above, left, right, before, was_below, was_above,
    own, to_left, to_right, to_below, to_above,
    towers, plates, tower_total, plate_total, *scratch,
):
    edge = edge_of(atoms.shape[0] // 4)
    fill(towers, 0, below, (0, 0, -edge), True)
    fill(towers, 1, atoms, (0, 0, 0), True)
    fill(towers, 2, above, (0, 0, edge), True)
    for along in range(3):
        fill(plates, along, left.at[along], (-edge, (along - 1) * edge, 0), False)
        fill(plates, 3 + along, right.at[along], (edge, (along - 1) * edge, 0), False)
    tower_total[0:192, :] = was_below[...]
    tower_total[192:384, :] = before[...]
    tower_total[384:576, :] = was_above[...]
    plate_total[...] = jnp.zeros_like(plate_total)
    across_count = listing[3 * SLOTS + 2]
    sweep(listing, 2 * SLOTS, 0, across_count, towers, plates, tower_total, plate_total, scratch)
    own[...] = tower_total[192:384, :]
    to_below[...] = tower_total[0:192, :]
    to_above[...] = tower_total[384:576, :]
    for along in range(3):
        to_left[along] = plate_total[along * 192 : along * 192 + 192, :]
        to_right[along] = plate_total[(3 + along) * 192 : (4 + along) * 192, :]


def fourth_kernel(listing, atoms, before, own, towers, plates, totals, *scratch):
    fill(towers, 0, atoms, (0, 0, 0), True)
    fill(plates, 0, atoms, (0, 0, 0), False)
    own[...] = before[...]
    totals[...] = jnp.zeros_like(totals)
    own_count = listing[3 * SLOTS]
    sweep(listing, 0, FIRST_OWN, own_count, towers, plates, own, totals, scratch)
    own[...] += totals[...]


def bond_kernel(atoms, velocities, inverse_mass, bond_partner, *refs):
    parts, (forces, moved) = refs[:-2], refs[-2:]
    rows = 8
    lane = lax.broadcasted_iota(jnp.int32, (rows, 128), 1)
    heads = lane - lane % 4
    corners = [heads + k for k in range(4)]

    def taken(values, index):
        return jnp.take_along_axis(values, index, axis=1)

    def step(tile, _):
        first = pl.multiple_of(tile * rows, rows)
        partner = bond_partner[pl.ds(first, rows), :]
        mass = inverse_mass[pl.ds(first, rows), :]
        hydro = partner != lane
        hits = [taken(partner, corner) == lane for corner in corners]
        bond, shift = [], []
        for c in range(3):
            place = pl.ds(c * 64 + first, rows)
            force = parts[0][place, :]
            for part in parts[1:]:
                force = force + part[place, :]
            forces[place, :] = force
            kicked = velocities[place, :] + TIME_STEP * FORCE_UNIT * mass * force
            shift.append(TIME_STEP * kicked)
            coords = atoms[place, :]
            bond.append(coords - taken(coords, partner))
        square = bond[0] * bond[0] + bond[1] * bond[1] + bond[2] * bond[2]
        paired = mass + taken(mass, partner)
        for sweep_number in range(ITERS):
            gap = [bond[c] + (shift[c] - taken(shift[c], partner)) for c in range(3)]
            excess = gap[0] * gap[0] + gap[1] * gap[1] + gap[2] * gap[2] - square
            along = gap[0] * bond[0] + gap[1] * bond[1] + gap[2] * bond[2]
            slope = 2.0 * along * paired
            factor = jnp.where(hydro, excess / jnp.where(hydro, slope, 1.0), 0.0)
            for c in range(3):
                delta = factor * bond[c]
                back = None
                for corner, hit in zip(corners, hits):
                    back = plus(back, jnp.where(hit, taken(delta, corner), 0.0))
                shift[c] = shift[c] + mass * (back - delta)
        for c in range(3):
            moved[pl.ds(c * 64 + first, rows), :] = shift[c] / TIME_STEP
        return 0

    lax.fori_loop(0, inverse_mass.shape[0] // rows, step, 0)


def planes(count=None):
    shape = (192, 128) if count is None else (count, 192, 128)
    return jax.ShapeDtypeStruct(shape, f32)


def run(kernel, outs, scalars, arrays, scratch, microseconds):
    smem = pl.BlockSpec(memory_space=pltpu.SMEM)
    vmem = pl.BlockSpec(memory_space=pltpu.VMEM)
    return pl.pallas_call(
        kernel,
        out_shape=outs,
        in_specs=[smem] * len(scalars) + [vmem] * len(arrays),
        out_specs=[smem if out.dtype == jnp.int32 else vmem for out in outs],
        scratch_shapes=scratch,
        compiler_params=pltpu.CompilerParams(vmem_limit_bytes=32 * 1024 * 1024),
        cost_estimate=pl.CostEstimate(
            flops=int(microseconds * 4e6), bytes_accessed=int(microseconds * 3e6), transcendentals=0
        ),
    )(*scalars, *arrays)


def local(atoms, velocities, inverse_mass, bond_partner, cluster_pairs, pair_count):
    own = atoms.reshape(256, 128)
    blocks = lambda count, rows: pltpu.VMEM((count * rows, 128), f32)
    back = passed_along(own, "gy", 1)
    ahead = passed_along(own, "gy", -1)
    below = passed_along(own, "gz", 1)
    above = passed_along(own, "gz", -1)
    triple = jnp.stack([back, own, ahead])
    left = passed_along(triple, "gx", 1)
    right = passed_along(triple, "gx", -1)
    listing, part = run(
        first_kernel,
        [jax.ShapeDtypeStruct((3 * SLOTS + 8,), jnp.int32), planes()],
        [cluster_pairs.reshape(2, -1), pair_count.reshape(1)],
        [own],
        [blocks(1, 256), blocks(1, 256), blocks(1, 192)] + sweep_scratch(),
        4,
    )
    part, to_back, to_ahead, to_below, to_above = run(
        second_kernel,
        [planes()] * 5,
        [listing],
        [own, back, ahead, below, above, part],
        [blocks(3, 256), blocks(3, 256), blocks(3, 192), blocks(3, 192)] + sweep_scratch(),
        6,
    )
    part, to_left, to_right, to_below, to_above = run(
        third_kernel,
        [planes(), planes(3), planes(3), planes(), planes()],
        [listing],
        [own, below, above, left, right, part, to_below, to_above],
        [blocks(3, 256), blocks(6, 256), blocks(3, 192), blocks(6, 192)] + sweep_scratch(),
        4,
    )
    from_right = passed_along(to_left, "gx", -1)
    from_left = passed_along(to_right, "gx", 1)
    from_above = passed_along(to_below, "gz", -1)
    from_below = passed_along(to_above, "gz", 1)
    (part,) = run(
        fourth_kernel,
        [planes()],
        [listing],
        [own, part],
        [blocks(1, 256), blocks(1, 256), blocks(1, 192)] + sweep_scratch(),
        6,
    )
    from_ahead = passed_along(to_back + from_left[0] + from_right[0], "gy", -1)
    from_back = passed_along(to_ahead + from_left[2] + from_right[2], "gy", 1)
    forces, moved = run(
        bond_kernel,
        [planes(), planes()],
        [],
        [
            own,
            velocities.reshape(192, 128),
            inverse_mass.reshape(64, 128),
            bond_partner.reshape(64, 128),
            part,
            from_left[1],
            from_right[1],
            from_above,
            from_below,
            from_ahead,
            from_back,
        ],
        [],
        2,
    )
    return (forces.reshape(3, 1, 1, 64, 128), moved.reshape(3, 1, 1, 64, 128))


def solution(mesh):
    return jax.shard_map(
        local,
        mesh=mesh,
        in_specs=(
            P(None, "gx", "gy", "gz", None),
            P(None, "gx", "gy", "gz", None),
            P("gx", "gy", "gz", None),
            P("gx", "gy", "gz", None),
            P(None, "gx", "gy", "gz"),
            P("gx", "gy", "gz"),
        ),
        out_specs=(P(None, "gx", "gy", "gz", None), P(None, "gx", "gy", "gz", None)),
        check_vma=False,
    )
```

```python
import functools

import jax
import jax.numpy as jnp
from jax import lax
from jax.experimental import pallas as pl
from jax.experimental.pallas import tpu as pltpu
from jax.sharding import PartitionSpec as P

ITERS = 2
TIME_STEP = 0.002
FORCE_UNIT = 500.0
CUTOFF = 1.2
SOFT_CORE = 0.04
SCALE = 1.0 / CUTOFF
CORE = SOFT_CORE / CUTOFF**2
STRENGTH = 1.0 / CUTOFF**2
HIGH, LOW = 8, 16
BLOCK = 2
SLOTS = 320
FIRST_OWN = 16
SECOND_GROUPS = 8
THIRD_OWN = 48
f32 = jnp.float32


def beside_of(place, count, outer):
    if not outer:
        return place ^ 1
    return (place + 1) % count if place % 2 else (place - 1) % count


def swapped(value, axis, outer):
    count = lax.axis_size(axis)
    pairs = [(source, beside_of(source, count, outer)) for source in range(count)]
    return lax.ppermute(value, axis, pairs)


def swapped_corner(value):
    columns, rows = lax.axis_size("gx"), lax.axis_size("gy")
    pairs = [
        (i * rows + j, beside_of(i, columns, True) * rows + beside_of(j, rows, False))
        for i in range(columns)
        for j in range(rows)
    ]
    return lax.ppermute(value, ("gx", "gy"), pairs)


def passed_along(value, axis, steps):
    count = lax.axis_size(axis)
    pairs = [(source, (source + steps) % count) for source in range(count)]
    return lax.ppermute(value, axis, pairs)


def plus(total, term):
    return term if total is None else total + term


def turned(value, shift):
    return value if shift % 128 == 0 else pltpu.roll(value, shift % 128, 1)


def eight_pairs(tower_planes, plate_planes, spun, pulled):
    tower_force = [None] * 3
    plate_force = [None] * 3
    rounds = HIGH // BLOCK
    for turn in range(rounds):
        coarse = [turn * BLOCK + u for u in range(BLOCK)]
        ahead = [[turned(v, -LOW * h) for v in tower_planes] for h in coarse]
        held = [[None] * 3 for _ in coarse]
        for low in range(LOW):
            if turn == 0:
                beside = [turned(v, low) for v in plate_planes]
                for c in range(4):
                    spun[low * 4 + c] = beside[c]
            else:
                beside = [spun[low * 4 + c] for c in range(4)]
            totals = [None if turn == 0 else pulled[low * 3 + c] for c in range(3)]
            for u in range(BLOCK):
                apart = [ahead[u][c] - beside[c] for c in range(3)]
                spread = apart[0] * apart[0] + apart[1] * apart[1] + apart[2] * apart[2]
                root = lax.rsqrt(spread + CORE)
                taper = jnp.maximum(1.0 - spread, 0.0)
                charges = ahead[u][3] * beside[3]
                scalar = (taper * taper) * charges * (root * root * root - 1.0)
                for c in range(3):
                    pull = scalar * apart[c]
                    held[u][c] = plus(held[u][c], pull)
                    totals[c] = plus(totals[c], pull)
            for c in range(3):
                if turn == rounds - 1:
                    plate_force[c] = plus(plate_force[c], turned(totals[c], -low))
                else:
                    pulled[low * 3 + c] = totals[c]
        for u, h in enumerate(coarse):
            for c in range(3):
                tower_force[c] = plus(tower_force[c], turned(held[u][c], LOW * h))
    return tower_force, plate_force


def sweep(listing, base, first, last, block, towers, plates, tower_total, plate_total, scratch):
    tower, plate, spun, pulled, tower_out, plate_out = scratch
    row = lax.broadcasted_iota(jnp.int32, (4, 128), 0)
    groups = (jnp.maximum(last - first, 0) + 7) // 8

    def slots(number):
        entry = listing[base + jnp.clip(number, first, last - 1)]
        t, p = entry >> 10, entry & 1023
        return t, p, (t >> 6) + block, (p >> 6) + block

    def fetch(group):
        for u in range(8):
            number = first + group * 8 + u
            t, p, tz, pz = slots(number)
            live = jnp.where(number < last, 1.0, 0.0)
            tower[pl.ds(u, 4, stride=8), :] = towers[
                pl.ds(tz * 256 + (t & 63), 4, stride=64), :
            ] * jnp.where(row == 3, live, 1.0)
            plate[pl.ds(u, 4, stride=8), :] = plates[
                pl.ds(pz * 256 + (p & 63), 4, stride=64), :
            ]

    def add_up(group):
        for u in range(8):
            t, p, tz, pz = slots(first + group * 8 + u)
            t, p = tz * 192 + (t & 63), pz * 192 + (p & 63)
            tower_total[pl.ds(t, 3, stride=64), :] += tower_out[pl.ds(u, 3, stride=8), :]
            plate_total[pl.ds(p, 3, stride=64), :] -= plate_out[pl.ds(u, 3, stride=8), :]

    def step(group, _):
        tower_planes = [tower[8 * c : 8 * c + 8, :] for c in range(4)]
        plate_planes = [plate[8 * c : 8 * c + 8, :] for c in range(4)]
        fetch(group + 1)
        add_up(group - 1)
        tower_force, plate_force = eight_pairs(tower_planes, plate_planes, spun, pulled)
        for c in range(3):
            tower_out[8 * c : 8 * c + 8, :] = tower_force[c]
            plate_out[8 * c : 8 * c + 8, :] = plate_force[c]
        return 0

    @pl.when(groups > 0)
    def _():
        tower_out[...] = jnp.zeros_like(tower_out)
        plate_out[...] = jnp.zeros_like(plate_out)
        fetch(0)
        lax.fori_loop(0, groups, step, 0)
        add_up(groups - 1)


def sweep_scratch():
    return [
        pltpu.VMEM((32, 128), f32),
        pltpu.VMEM((32, 128), f32),
        pltpu.VMEM((4 * LOW, 8, 128), f32),
        pltpu.VMEM((3 * LOW, 8, 128), f32),
        pltpu.VMEM((24, 128), f32),
        pltpu.VMEM((24, 128), f32),
    ]


def fill(target, block, source, lifts, strength):
    for c in range(4):
        start = block * 256 + c * 64
        values = source[c * 64 : c * 64 + 64, :]
        if c < 3:
            values = values * SCALE if isinstance(lifts[c], int) else (values + lifts[c]) * SCALE
        elif strength:
            values = values * STRENGTH
        target[start : start + 64, :] = values


def edge_of(clusters):
    return 2.4 * (clusters / 8.0) ** (1.0 / 3.0)


def sort_pairs(pairs, live, side, listing, order):
    for block in range(9):
        dx, dy = block // 3 - 1, block % 3 - 1
        if dx == 0:
            place = 1 - dy * side[1]
        else:
            place = jnp.where(side[0] == dx, 0, 3)
            if dy:
                place = place + jnp.where(side[1] == dy, 1, 2)
        order[block] = place * 64

    def step(chunk, taken):
        for u in range(8):
            number = chunk * 8 + u
            t, p = pairs[0, number], pairs[1, number]
            block = p >> 6
            across = jnp.logical_or(p < 192, p >= 384)
            home = jnp.logical_and((t >> 6) == 1, block == 4)
            entry = jnp.where(home, t & 63, t) << 10
            entry = entry | (jnp.where(home, 0, order[block]) + (p & 63))
            shift = jnp.where(home, 0, jnp.where(across, 20, 10))
            place = (shift << 5) + ((taken >> shift) & 1023)
            dead = number >= live
            listing[jnp.where(dead, 3 * SLOTS + 7, place)] = entry
            taken = taken + jnp.where(dead, 0, jnp.int32(1) << shift)
        return taken

    taken = lax.fori_loop(0, (live + 7) // 8, step, jnp.int32(0))
    for kind in range(3):
        listing[3 * SLOTS + kind] = (taken >> (10 * kind)) & 1023
    for axis in range(2):
        listing[3 * SLOTS + 3 + axis] = side[axis]


def edges(listing, atoms):
    edge = edge_of(atoms.shape[0] // 4)
    signs = [listing[3 * SLOTS + 3 + axis].astype(f32) for axis in range(2)]
    return signs[0] * edge, signs[1] * edge, edge


def own_end(listing, stage):
    own_count = listing[3 * SLOTS]
    flat_groups = (listing[3 * SLOTS + 1] + 7) // 8
    second = FIRST_OWN + jnp.maximum(SECOND_GROUPS - flat_groups, 0) * 8
    ends = [0, FIRST_OWN, second, second + THIRD_OWN, 2 * SLOTS]
    return jnp.minimum(own_count, ends[stage])


def first_kernel(
    pairs, count, side, atoms, listing, own, order, towers, plates, totals, *scratch
):
    fill(towers, 0, atoms, (0, 0, 0), True)
    fill(plates, 0, atoms, (0, 0, 0), False)
    own[...] = jnp.zeros_like(own)
    totals[...] = jnp.zeros_like(totals)
    sort_pairs(pairs, count[0], side, listing, order)
    sweep(listing, 0, 0, own_end(listing, 1), 0, towers, plates, own, totals, scratch)
    own[...] += totals[...]


def second_kernel(
    listing, atoms, inner, outer, below, above, before,
    own, to_inner, to_outer, to_below, to_above,
    towers, plates, tower_total, plate_total, *scratch,
):
    _, along, edge = edges(listing, atoms)
    fill(towers, 0, below, (0, 0, -edge), True)
    fill(towers, 1, atoms, (0, 0, 0), True)
    fill(towers, 2, above, (0, 0, edge), True)
    fill(plates, 0, inner, (0, along, 0), False)
    fill(plates, 1, atoms, (0, 0, 0), False)
    fill(plates, 2, outer, (0, -along, 0), False)
    tower_total[...] = jnp.zeros_like(tower_total)
    plate_total[...] = jnp.zeros_like(plate_total)
    shared = (towers, plates, tower_total, plate_total, scratch)
    sweep(listing, SLOTS, 0, listing[3 * SLOTS + 1], 0, *shared)
    sweep(listing, 0, own_end(listing, 1), own_end(listing, 2), 1, *shared)
    own[...] = before[...] + tower_total[192:384, :] + plate_total[192:384, :]
    to_below[...] = tower_total[0:192, :]
    to_above[...] = tower_total[384:576, :]
    to_inner[...] = plate_total[0:192, :]
    to_outer[...] = plate_total[384:576, :]


def third_kernel(
    listing, atoms, below, above, mate, mate_inner, mate_outer, far, corner, far_outer,
    before, was_below, was_above,
    own, to_mate, to_far, to_corner, to_below, to_above,
    towers, plates, tower_total, plate_total, *scratch,
):
    across, along, edge = edges(listing, atoms)
    fill(towers, 0, below, (0, 0, -edge), True)
    fill(towers, 1, atoms, (0, 0, 0), True)
    fill(towers, 2, above, (0, 0, edge), True)
    fill(plates, 0, mate, (across, 0, 0), False)
    fill(plates, 1, mate_inner, (across, along, 0), False)
    fill(plates, 2, mate_outer, (across, -along, 0), False)
    fill(plates, 3, far, (-across, 0, 0), False)
    fill(plates, 4, corner, (-across, along, 0), False)
    fill(plates, 5, far_outer, (-across, -along, 0), False)
    tower_total[0:192, :] = was_below[...]
    tower_total[192:384, :] = before[...]
    tower_total[384:576, :] = was_above[...]
    plate_total[...] = jnp.zeros_like(plate_total)
    across_count = listing[3 * SLOTS + 2]
    shared = (towers, plates, tower_total, plate_total, scratch)
    sweep(listing, 2 * SLOTS, 0, across_count, 0, *shared)
    own[...] = tower_total[192:384, :]
    to_below[...] = tower_total[0:192, :]
    to_above[...] = tower_total[384:576, :]
    to_mate[...] = plate_total[0:576, :]
    to_far[0:192, :] = plate_total[576:768, :]
    to_far[192:384, :] = plate_total[960:1152, :]
    to_corner[...] = plate_total[768:960, :]


def own_kernel(stage, listing, atoms, before, own, towers, plates, totals, *scratch):
    fill(towers, 0, atoms, (0, 0, 0), True)
    fill(plates, 0, atoms, (0, 0, 0), False)
    own[...] = before[...]
    totals[...] = jnp.zeros_like(totals)
    shared = (towers, plates, own, totals, scratch)
    sweep(listing, 0, own_end(listing, stage - 1), own_end(listing, stage), 0, *shared)
    own[...] += totals[...]


def bond_kernel(atoms, velocities, inverse_mass, bond_partner, *refs):
    parts, (forces, moved) = refs[:-2], refs[-2:]
    rows = inverse_mass.shape[0]
    lane = lax.broadcasted_iota(jnp.int32, (rows, 128), 1)
    heads = lane - lane % 4
    corners = [heads + k for k in range(4)]

    def taken(values, index):
        return jnp.take_along_axis(values, index, axis=1)

    partner = bond_partner[...]
    mass = inverse_mass[...]
    hydro = partner != lane
    hits = [taken(partner, corner) == lane for corner in corners]
    bond, shift = [], []
    for c in range(3):
        place = slice(c * rows, c * rows + rows)
        force = parts[0][place, :]
        for part in parts[1:]:
            force = force + part[place, :]
        forces[place, :] = force
        kicked = velocities[place, :] + TIME_STEP * FORCE_UNIT * mass * force
        shift.append(TIME_STEP * kicked)
        coords = atoms[place, :]
        bond.append(coords - taken(coords, partner))
    square = bond[0] * bond[0] + bond[1] * bond[1] + bond[2] * bond[2]
    paired = mass + taken(mass, partner)
    for _ in range(ITERS):
        gap = [bond[c] + (shift[c] - taken(shift[c], partner)) for c in range(3)]
        excess = gap[0] * gap[0] + gap[1] * gap[1] + gap[2] * gap[2] - square
        along = gap[0] * bond[0] + gap[1] * bond[1] + gap[2] * bond[2]
        slope = 2.0 * along * paired
        factor = jnp.where(hydro, excess / jnp.where(hydro, slope, 1.0), 0.0)
        for c in range(3):
            delta = factor * bond[c]
            back = None
            for corner, hit in zip(corners, hits):
                back = plus(back, jnp.where(hit, taken(delta, corner), 0.0))
            shift[c] = shift[c] + mass * (back - delta)
    for c in range(3):
        moved[c * rows : c * rows + rows, :] = shift[c] / TIME_STEP


def planes(count=1):
    return jax.ShapeDtypeStruct((count * 192, 128), f32)


def run(kernel, outs, scalars, arrays, scratch, microseconds):
    smem = pl.BlockSpec(memory_space=pltpu.SMEM)
    vmem = pl.BlockSpec(memory_space=pltpu.VMEM)
    return pl.pallas_call(
        kernel,
        out_shape=outs,
        in_specs=[smem] * len(scalars) + [vmem] * len(arrays),
        out_specs=[smem if out.dtype == jnp.int32 else vmem for out in outs],
        scratch_shapes=scratch,
        compiler_params=pltpu.CompilerParams(vmem_limit_bytes=32 * 1024 * 1024),
        cost_estimate=pl.CostEstimate(
            flops=int(microseconds * 4e6), bytes_accessed=int(microseconds * 3e6), transcendentals=0
        ),
    )(*scalars, *arrays)


def local(atoms, velocities, inverse_mass, bond_partner, cluster_pairs, pair_count):
    own = atoms.reshape(256, 128)
    blocks = lambda count, rows: pltpu.VMEM((count * rows, 128), f32)
    inner = swapped(own, "gy", False)
    outer = swapped(own, "gy", True)
    below = passed_along(own, "gz", 1)
    above = passed_along(own, "gz", -1)
    far = swapped(own, "gx", True)
    corner = swapped_corner(own)
    mate = swapped(own, "gx", False)
    side = jnp.stack([1 - 2 * (lax.axis_index(axis) % 2) for axis in ("gx", "gy")])
    listing, part = run(
        first_kernel,
        [jax.ShapeDtypeStruct((3 * SLOTS + 8,), jnp.int32), planes()],
        [cluster_pairs.reshape(2, -1), pair_count.reshape(1), side.astype(jnp.int32)],
        [own],
        [pltpu.SMEM((16,), jnp.int32)]
        + [blocks(1, 256), blocks(1, 256), blocks(1, 192)]
        + sweep_scratch(),
        4,
    )
    inner, outer, below, above, far, corner, mate, part = lax.optimization_barrier(
        (inner, outer, below, above, far, corner, mate, part)
    )
    far_outer = swapped(outer, "gx", True)
    mate_inner = swapped(inner, "gx", False)
    mate_outer = swapped(outer, "gx", False)
    part, to_inner, to_outer, to_below, to_above = run(
        second_kernel,
        [planes()] * 5,
        [listing],
        [own, inner, outer, below, above, part],
        [blocks(3, 256), blocks(3, 256), blocks(3, 192), blocks(3, 192)] + sweep_scratch(),
        6,
    )
    part, to_mate, to_far, to_corner, to_below, to_above = run(
        third_kernel,
        [planes(), planes(3), planes(2), planes(), planes(), planes()],
        [listing],
        [own, below, above, mate, mate_inner, mate_outer, far, corner, far_outer]
        + [part, to_below, to_above],
        [blocks(3, 256), blocks(6, 256), blocks(3, 192), blocks(6, 192)] + sweep_scratch(),
        4,
    )
    from_mate = swapped(to_mate, "gx", False)
    from_far = swapped(to_far, "gx", True)
    from_corner = swapped_corner(to_corner)
    from_above = passed_along(to_below, "gz", -1)
    from_below = passed_along(to_above, "gz", 1)
    own_scratch = [blocks(1, 256), blocks(1, 256), blocks(1, 192)] + sweep_scratch()
    (part,) = run(
        functools.partial(own_kernel, 3), [planes()], [listing], [own, part], own_scratch, 5
    )
    to_inner = to_inner + from_mate[192:384]
    to_outer = to_outer + from_mate[384:576] + from_far[192:384]
    to_inner, to_outer, part = lax.optimization_barrier((to_inner, to_outer, part))
    from_inner = swapped(to_inner, "gy", False)
    from_outer = swapped(to_outer, "gy", True)
    (part,) = run(
        functools.partial(own_kernel, 4), [planes()], [listing], [own, part], own_scratch, 4
    )
    forces, moved = run(
        bond_kernel,
        [planes(), planes()],
        [],
        [
            own,
            velocities.reshape(192, 128),
            inverse_mass.reshape(64, 128),
            bond_partner.reshape(64, 128),
            part,
            from_mate,
            from_far,
            from_corner,
            from_above,
            from_below,
            from_inner,
            from_outer,
        ],
        [],
        2,
    )
    return (forces.reshape(3, 1, 1, 64, 128), moved.reshape(3, 1, 1, 64, 128))


def solution(mesh):
    return jax.shard_map(
        local,
        mesh=mesh,
        in_specs=(
            P(None, "gx", "gy", "gz", None),
            P(None, "gx", "gy", "gz", None),
            P("gx", "gy", "gz", None),
            P("gx", "gy", "gz", None),
            P(None, "gx", "gy", "gz"),
            P("gx", "gy", "gz"),
        ),
        out_specs=(P(None, "gx", "gy", "gz", None), P(None, "gx", "gy", "gz", None)),
        check_vma=False,
    )
```

```python
import functools

import jax
import jax.numpy as jnp
from jax import lax
from jax.experimental import pallas as pl
from jax.experimental.pallas import tpu as pltpu
from jax.sharding import PartitionSpec as P

ITERS = 2
TIME_STEP = 0.002
FORCE_UNIT = 500.0
CUTOFF = 1.2
SOFT_CORE = 0.04
SCALE = 1.0 / CUTOFF
CORE = SOFT_CORE / CUTOFF**2
STRENGTH = 1.0 / CUTOFF**2
HIGH, LOW = 8, 16
BLOCK = 2
SLOTS = 320
FIRST_OWN = 16
SECOND_GROUPS = 8
THIRD_OWN = 48
f32 = jnp.float32


def beside_of(place, count, outer):
    if not outer:
        return place ^ 1
    return (place + 1) % count if place % 2 else (place - 1) % count


def swapped(value, axis, outer):
    count = lax.axis_size(axis)
    pairs = [(source, beside_of(source, count, outer)) for source in range(count)]
    return lax.ppermute(value, axis, pairs)


def swapped_corner(value):
    columns, rows = lax.axis_size("gx"), lax.axis_size("gy")
    pairs = [
        (i * rows + j, beside_of(i, columns, True) * rows + beside_of(j, rows, False))
        for i in range(columns)
        for j in range(rows)
    ]
    return lax.ppermute(value, ("gx", "gy"), pairs)


def plus(total, term):
    return term if total is None else total + term


def turned(value, shift):
    return value if shift % 128 == 0 else pltpu.roll(value, shift % 128, 1)


def eight_pairs(tower_planes, plate_planes, spun, pulled):
    tower_force = [None] * 3
    plate_force = [None] * 3
    rounds = HIGH // BLOCK
    for turn in range(rounds):
        coarse = [turn * BLOCK + u for u in range(BLOCK)]
        ahead = [[turned(v, -LOW * h) for v in tower_planes] for h in coarse]
        held = [[None] * 3 for _ in coarse]
        for low in range(LOW):
            if turn == 0:
                beside = [turned(v, low) for v in plate_planes]
                for c in range(4):
                    spun[low * 4 + c] = beside[c]
            else:
                beside = [spun[low * 4 + c] for c in range(4)]
            totals = [None if turn == 0 else pulled[low * 3 + c] for c in range(3)]
            for u in range(BLOCK):
                apart = [ahead[u][c] - beside[c] for c in range(3)]
                spread = apart[0] * apart[0] + apart[1] * apart[1] + apart[2] * apart[2]
                root = lax.rsqrt(spread + CORE)
                taper = jnp.maximum(1.0 - spread, 0.0)
                charges = ahead[u][3] * beside[3]
                scalar = (taper * taper) * charges * (root * root * root - 1.0)
                for c in range(3):
                    pull = scalar * apart[c]
                    held[u][c] = plus(held[u][c], pull)
                    totals[c] = plus(totals[c], pull)
            for c in range(3):
                if turn == rounds - 1:
                    plate_force[c] = plus(plate_force[c], turned(totals[c], -low))
                else:
                    pulled[low * 3 + c] = totals[c]
        for u, h in enumerate(coarse):
            for c in range(3):
                tower_force[c] = plus(tower_force[c], turned(held[u][c], LOW * h))
    return tower_force, plate_force


def sweep(listing, base, first, last, block, towers, plates, tower_total, plate_total, scratch):
    tower, plate, spun, pulled, tower_out, plate_out = scratch
    row = lax.broadcasted_iota(jnp.int32, (4, 128), 0)
    groups = (jnp.maximum(last - first, 0) + 7) // 8

    def slots(number):
        entry = listing[base + jnp.clip(number, first, last - 1)]
        t, p = entry >> 10, entry & 1023
        return t, p, (t >> 6) + block, (p >> 6) + block

    def fetch(group):
        for u in range(8):
            number = first + group * 8 + u
            t, p, tz, pz = slots(number)
            live = jnp.where(number < last, 1.0, 0.0)
            tower[pl.ds(u, 4, stride=8), :] = towers[
                pl.ds(tz * 256 + (t & 63), 4, stride=64), :
            ] * jnp.where(row == 3, live, 1.0)
            plate[pl.ds(u, 4, stride=8), :] = plates[
                pl.ds(pz * 256 + (p & 63), 4, stride=64), :
            ]

    def add_up(group):
        for u in range(8):
            t, p, tz, pz = slots(first + group * 8 + u)
            t, p = tz * 192 + (t & 63), pz * 192 + (p & 63)
            tower_total[pl.ds(t, 3, stride=64), :] += tower_out[pl.ds(u, 3, stride=8), :]
            plate_total[pl.ds(p, 3, stride=64), :] -= plate_out[pl.ds(u, 3, stride=8), :]

    def step(group, _):
        tower_planes = [tower[8 * c : 8 * c + 8, :] for c in range(4)]
        plate_planes = [plate[8 * c : 8 * c + 8, :] for c in range(4)]
        fetch(group + 1)
        add_up(group - 1)
        tower_force, plate_force = eight_pairs(tower_planes, plate_planes, spun, pulled)
        for c in range(3):
            tower_out[8 * c : 8 * c + 8, :] = tower_force[c]
            plate_out[8 * c : 8 * c + 8, :] = plate_force[c]
        return 0

    @pl.when(groups > 0)
    def _():
        tower_out[...] = jnp.zeros_like(tower_out)
        plate_out[...] = jnp.zeros_like(plate_out)
        fetch(0)
        lax.fori_loop(0, groups, step, 0)
        add_up(groups - 1)


def sweep_scratch():
    return [
        pltpu.VMEM((32, 128), f32),
        pltpu.VMEM((32, 128), f32),
        pltpu.VMEM((4 * LOW, 8, 128), f32),
        pltpu.VMEM((3 * LOW, 8, 128), f32),
        pltpu.VMEM((24, 128), f32),
        pltpu.VMEM((24, 128), f32),
    ]


def fill(target, block, source, lifts, strength):
    for c in range(4):
        start = block * 256 + c * 64
        values = source[c * 64 : c * 64 + 64, :]
        if c < 3:
            values = values * SCALE if isinstance(lifts[c], int) else (values + lifts[c]) * SCALE
        elif strength:
            values = values * STRENGTH
        target[start : start + 64, :] = values


def edge_of(clusters):
    return 2.4 * (clusters / 8.0) ** (1.0 / 3.0)


def sort_pairs(pairs, live, side, listing, order):
    for block in range(9):
        dx, dy = block // 3 - 1, block % 3 - 1
        if dx == 0:
            place = 1 - dy * side[1]
        else:
            place = jnp.where(side[0] == dx, 0, 3)
            if dy:
                place = place + jnp.where(side[1] == dy, 1, 2)
        order[block] = place * 64

    def step(chunk, taken):
        for u in range(8):
            number = chunk * 8 + u
            t, p = pairs[0, number], pairs[1, number]
            block = p >> 6
            across = jnp.logical_or(p < 192, p >= 384)
            home = jnp.logical_and((t >> 6) == 1, block == 4)
            entry = jnp.where(home, t & 63, jnp.where(side[2] > 0, t, (t & 63) + 128 - (t & 192))) << 10
            entry = entry | (jnp.where(home, 0, order[block]) + (p & 63))
            shift = jnp.where(home, 0, jnp.where(across, 20, 10))
            place = (shift << 5) + ((taken >> shift) & 1023)
            dead = number >= live
            listing[jnp.where(dead, 3 * SLOTS + 7, place)] = entry
            taken = taken + jnp.where(dead, 0, jnp.int32(1) << shift)
        return taken

    taken = lax.fori_loop(0, (live + 7) // 8, step, jnp.int32(0))
    for kind in range(3):
        listing[3 * SLOTS + kind] = (taken >> (10 * kind)) & 1023
    for axis in range(3):
        listing[3 * SLOTS + 3 + axis] = side[axis]


def edges(listing, atoms):
    edge = edge_of(atoms.shape[0] // 4)
    return [listing[3 * SLOTS + 3 + axis].astype(f32) * edge for axis in range(3)]


def own_end(listing, stage):
    own_count = listing[3 * SLOTS]
    flat_groups = (listing[3 * SLOTS + 1] + 7) // 8
    second = FIRST_OWN + jnp.maximum(SECOND_GROUPS - flat_groups, 0) * 8
    ends = [0, FIRST_OWN, second, second + THIRD_OWN, 2 * SLOTS]
    return jnp.minimum(own_count, ends[stage])


def first_kernel(
    pairs, count, side, atoms, listing, own, order, towers, plates, totals, *scratch
):
    fill(towers, 0, atoms, (0, 0, 0), True)
    fill(plates, 0, atoms, (0, 0, 0), False)
    own[...] = jnp.zeros_like(own)
    totals[...] = jnp.zeros_like(totals)
    sort_pairs(pairs, count[0], side, listing, order)
    sweep(listing, 0, 0, own_end(listing, 1), 0, towers, plates, own, totals, scratch)
    own[...] += totals[...]


def second_kernel(
    listing, atoms, inner, outer, under, over, before,
    own, to_inner, to_outer, to_under, to_over,
    towers, plates, tower_total, plate_total, *scratch,
):
    _, along, up = edges(listing, atoms)
    fill(towers, 0, under, (0, 0, -up), True)
    fill(towers, 1, atoms, (0, 0, 0), True)
    fill(towers, 2, over, (0, 0, up), True)
    fill(plates, 0, inner, (0, along, 0), False)
    fill(plates, 1, atoms, (0, 0, 0), False)
    fill(plates, 2, outer, (0, -along, 0), False)
    tower_total[...] = jnp.zeros_like(tower_total)
    plate_total[...] = jnp.zeros_like(plate_total)
    shared = (towers, plates, tower_total, plate_total, scratch)
    sweep(listing, SLOTS, 0, listing[3 * SLOTS + 1], 0, *shared)
    sweep(listing, 0, own_end(listing, 1), own_end(listing, 2), 1, *shared)
    own[...] = before[...] + tower_total[192:384, :] + plate_total[192:384, :]
    to_under[...] = tower_total[0:192, :]
    to_over[...] = tower_total[384:576, :]
    to_inner[...] = plate_total[0:192, :]
    to_outer[...] = plate_total[384:576, :]


def third_kernel(
    listing, atoms, under, over, mate, mate_inner, mate_outer, far, corner, far_outer,
    before, was_under, was_over,
    own, to_mate, to_far, to_corner, to_under, to_over,
    towers, plates, tower_total, plate_total, *scratch,
):
    across, along, up = edges(listing, atoms)
    fill(towers, 0, under, (0, 0, -up), True)
    fill(towers, 1, atoms, (0, 0, 0), True)
    fill(towers, 2, over, (0, 0, up), True)
    fill(plates, 0, mate, (across, 0, 0), False)
    fill(plates, 1, mate_inner, (across, along, 0), False)
    fill(plates, 2, mate_outer, (across, -along, 0), False)
    fill(plates, 3, far, (-across, 0, 0), False)
    fill(plates, 4, corner, (-across, along, 0), False)
    fill(plates, 5, far_outer, (-across, -along, 0), False)
    tower_total[0:192, :] = was_under[...]
    tower_total[192:384, :] = before[...]
    tower_total[384:576, :] = was_over[...]
    plate_total[...] = jnp.zeros_like(plate_total)
    across_count = listing[3 * SLOTS + 2]
    shared = (towers, plates, tower_total, plate_total, scratch)
    sweep(listing, 2 * SLOTS, 0, across_count, 0, *shared)
    own[...] = tower_total[192:384, :]
    to_under[...] = tower_total[0:192, :]
    to_over[...] = tower_total[384:576, :]
    to_mate[...] = plate_total[0:576, :]
    to_far[0:192, :] = plate_total[576:768, :]
    to_far[192:384, :] = plate_total[960:1152, :]
    to_corner[...] = plate_total[768:960, :]


def own_kernel(stage, listing, atoms, before, own, towers, plates, totals, *scratch):
    fill(towers, 0, atoms, (0, 0, 0), True)
    fill(plates, 0, atoms, (0, 0, 0), False)
    own[...] = before[...]
    totals[...] = jnp.zeros_like(totals)
    shared = (towers, plates, own, totals, scratch)
    sweep(listing, 0, own_end(listing, stage - 1), own_end(listing, stage), 0, *shared)
    own[...] += totals[...]


def bond_kernel(atoms, velocities, inverse_mass, bond_partner, *refs):
    parts, (forces, moved) = refs[:-2], refs[-2:]
    rows = inverse_mass.shape[0]
    lane = lax.broadcasted_iota(jnp.int32, (rows, 128), 1)
    heads = lane - lane % 4
    corners = [heads + k for k in range(4)]

    def taken(values, index):
        return jnp.take_along_axis(values, index, axis=1)

    partner = bond_partner[...]
    mass = inverse_mass[...]
    hydro = partner != lane
    hits = [taken(partner, corner) == lane for corner in corners]
    bond, shift = [], []
    for c in range(3):
        place = slice(c * rows, c * rows + rows)
        force = parts[0][place, :]
        for part in parts[1:]:
            force = force + part[place, :]
        forces[place, :] = force
        kicked = velocities[place, :] + TIME_STEP * FORCE_UNIT * mass * force
        shift.append(TIME_STEP * kicked)
        coords = atoms[place, :]
        bond.append(coords - taken(coords, partner))
    square = bond[0] * bond[0] + bond[1] * bond[1] + bond[2] * bond[2]
    paired = mass + taken(mass, partner)
    for _ in range(ITERS):
        gap = [bond[c] + (shift[c] - taken(shift[c], partner)) for c in range(3)]
        excess = gap[0] * gap[0] + gap[1] * gap[1] + gap[2] * gap[2] - square
        along = gap[0] * bond[0] + gap[1] * bond[1] + gap[2] * bond[2]
        slope = 2.0 * along * paired
        factor = jnp.where(hydro, excess / jnp.where(hydro, slope, 1.0), 0.0)
        for c in range(3):
            delta = factor * bond[c]
            back = None
            for corner, hit in zip(corners, hits):
                back = plus(back, jnp.where(hit, taken(delta, corner), 0.0))
            shift[c] = shift[c] + mass * (back - delta)
    for c in range(3):
        moved[c * rows : c * rows + rows, :] = shift[c] / TIME_STEP


def planes(count=1):
    return jax.ShapeDtypeStruct((count * 192, 128), f32)


def run(kernel, outs, scalars, arrays, scratch, microseconds):
    smem = pl.BlockSpec(memory_space=pltpu.SMEM)
    vmem = pl.BlockSpec(memory_space=pltpu.VMEM)
    return pl.pallas_call(
        kernel,
        out_shape=outs,
        in_specs=[smem] * len(scalars) + [vmem] * len(arrays),
        out_specs=[smem if out.dtype == jnp.int32 else vmem for out in outs],
        scratch_shapes=scratch,
        compiler_params=pltpu.CompilerParams(vmem_limit_bytes=32 * 1024 * 1024),
        cost_estimate=pl.CostEstimate(
            flops=int(microseconds * 4e6), bytes_accessed=int(microseconds * 3e6), transcendentals=0
        ),
    )(*scalars, *arrays)


def local(atoms, velocities, inverse_mass, bond_partner, cluster_pairs, pair_count):
    own = atoms.reshape(256, 128)
    blocks = lambda count, rows: pltpu.VMEM((count * rows, 128), f32)
    inner = swapped(own, "gy", False)
    outer = swapped(own, "gy", True)
    under = swapped(own, "gz", True)
    over = swapped(own, "gz", False)
    far = swapped(own, "gx", True)
    corner = swapped_corner(own)
    mate = swapped(own, "gx", False)
    side = jnp.stack([1 - 2 * (lax.axis_index(axis) % 2) for axis in ("gx", "gy", "gz")])
    listing, part = run(
        first_kernel,
        [jax.ShapeDtypeStruct((3 * SLOTS + 8,), jnp.int32), planes()],
        [cluster_pairs.reshape(2, -1), pair_count.reshape(1), side.astype(jnp.int32)],
        [own],
        [pltpu.SMEM((16,), jnp.int32)]
        + [blocks(1, 256), blocks(1, 256), blocks(1, 192)]
        + sweep_scratch(),
        4,
    )
    corner, over, under, inner, outer, far, mate, part = lax.optimization_barrier(
        (corner, over, under, inner, outer, far, mate, part)
    )
    far_outer = swapped(outer, "gx", True)
    mate_inner = swapped(inner, "gx", False)
    mate_outer = swapped(outer, "gx", False)
    part, to_inner, to_outer, to_under, to_over = run(
        second_kernel,
        [planes()] * 5,
        [listing],
        [own, inner, outer, under, over, part],
        [blocks(3, 256), blocks(3, 256), blocks(3, 192), blocks(3, 192)] + sweep_scratch(),
        6,
    )
    part, to_mate, to_far, to_corner, to_under, to_over = run(
        third_kernel,
        [planes(), planes(3), planes(2), planes(), planes(), planes()],
        [listing],
        [own, under, over, mate, mate_inner, mate_outer, far, corner, far_outer]
        + [part, to_under, to_over],
        [blocks(3, 256), blocks(6, 256), blocks(3, 192), blocks(6, 192)] + sweep_scratch(),
        4,
    )
    from_mate = swapped(to_mate, "gx", False)
    from_far = swapped(to_far, "gx", True)
    from_corner = swapped_corner(to_corner)
    from_under = swapped(to_under, "gz", True)
    from_over = swapped(to_over, "gz", False)
    own_scratch = [blocks(1, 256), blocks(1, 256), blocks(1, 192)] + sweep_scratch()
    (part,) = run(
        functools.partial(own_kernel, 3), [planes()], [listing], [own, part], own_scratch, 5
    )
    to_inner = to_inner + from_mate[192:384]
    to_outer = to_outer + from_mate[384:576] + from_far[192:384]
    to_inner, to_outer, part = lax.optimization_barrier((to_inner, to_outer, part))
    from_inner = swapped(to_inner, "gy", False)
    from_outer = swapped(to_outer, "gy", True)
    (part,) = run(
        functools.partial(own_kernel, 4), [planes()], [listing], [own, part], own_scratch, 4
    )
    forces, moved = run(
        bond_kernel,
        [planes(), planes()],
        [],
        [
            own,
            velocities.reshape(192, 128),
            inverse_mass.reshape(64, 128),
            bond_partner.reshape(64, 128),
            part,
            from_mate,
            from_far,
            from_corner,
            from_over,
            from_under,
            from_inner,
            from_outer,
        ],
        [],
        2,
    )
    return (forces.reshape(3, 1, 1, 64, 128), moved.reshape(3, 1, 1, 64, 128))


def solution(mesh):
    return jax.shard_map(
        local,
        mesh=mesh,
        in_specs=(
            P(None, "gx", "gy", "gz", None),
            P(None, "gx", "gy", "gz", None),
            P("gx", "gy", "gz", None),
            P("gx", "gy", "gz", None),
            P(None, "gx", "gy", "gz"),
            P("gx", "gy", "gz"),
        ),
        out_specs=(P(None, "gx", "gy", "gz", None), P(None, "gx", "gy", "gz", None)),
        check_vma=False,
    )
```

```python
import functools

import jax
import jax.numpy as jnp
from jax import lax
from jax.experimental import pallas as pl
from jax.experimental.pallas import tpu as pltpu
from jax.sharding import PartitionSpec as P

ITERS = 2
TIME_STEP = 0.002
FORCE_UNIT = 500.0
CUTOFF = 1.2
SOFT_CORE = 0.04
SCALE = 1.0 / CUTOFF
CORE = SOFT_CORE / CUTOFF**2
STRENGTH = 1.0 / CUTOFF**2
HIGH, LOW = 8, 16
BLOCK = 2
SLOTS = 320
FIRST_OWN = 16
SECOND_GROUPS = 8
THIRD_OWN = 48
f32 = jnp.float32


def beside_of(place, count, outer):
    if not outer:
        return place ^ 1
    return (place + 1) % count if place % 2 else (place - 1) % count


def swapped(value, axis, outer):
    count = lax.axis_size(axis)
    pairs = [(source, beside_of(source, count, outer)) for source in range(count)]
    return lax.ppermute(value, axis, pairs)


def swapped_corner(value):
    columns, rows = lax.axis_size("gx"), lax.axis_size("gy")
    pairs = [
        (i * rows + j, beside_of(i, columns, True) * rows + beside_of(j, rows, False))
        for i in range(columns)
        for j in range(rows)
    ]
    return lax.ppermute(value, ("gx", "gy"), pairs)


def plus(total, term):
    return term if total is None else total + term


def turned(value, shift):
    return value if shift % 128 == 0 else pltpu.roll(value, shift % 128, 1)


def eight_pairs(tower_planes, plate_planes, spun, pulled):
    tower_force = [None] * 3
    plate_force = [None] * 3
    rounds = HIGH // BLOCK
    for turn in range(rounds):
        coarse = [turn * BLOCK + u for u in range(BLOCK)]
        ahead = [[turned(v, -LOW * h) for v in tower_planes] for h in coarse]
        held = [[None] * 3 for _ in coarse]
        for low in range(LOW):
            if turn == 0:
                beside = [turned(v, low) for v in plate_planes]
                for c in range(4):
                    spun[low * 4 + c] = beside[c]
            else:
                beside = [spun[low * 4 + c] for c in range(4)]
            totals = [None if turn == 0 else pulled[low * 3 + c] for c in range(3)]
            for u in range(BLOCK):
                apart = [ahead[u][c] - beside[c] for c in range(3)]
                spread = apart[0] * apart[0] + apart[1] * apart[1] + apart[2] * apart[2]
                root = lax.rsqrt(spread + CORE)
                taper = jnp.maximum(1.0 - spread, 0.0)
                charges = ahead[u][3] * beside[3]
                scalar = (taper * taper) * charges * (root * root * root - 1.0)
                for c in range(3):
                    pull = scalar * apart[c]
                    held[u][c] = plus(held[u][c], pull)
                    totals[c] = plus(totals[c], pull)
            for c in range(3):
                if turn == rounds - 1:
                    plate_force[c] = plus(plate_force[c], turned(totals[c], -low))
                else:
                    pulled[low * 3 + c] = totals[c]
        for u, h in enumerate(coarse):
            for c in range(3):
                tower_force[c] = plus(tower_force[c], turned(held[u][c], LOW * h))
    return tower_force, plate_force


def sweep(listing, base, first, last, block, towers, plates, tower_total, plate_total, scratch):
    tower, plate, spun, pulled, tower_out, plate_out = scratch
    row = lax.broadcasted_iota(jnp.int32, (4, 128), 0)
    groups = (jnp.maximum(last - first, 0) + 7) // 8

    def slots(number):
        entry = listing[base + jnp.clip(number, first, last - 1)]
        t, p = entry >> 10, entry & 1023
        return t, p, (t >> 6) + block, (p >> 6) + block

    def fetch(group):
        for u in range(8):
            number = first + group * 8 + u
            t, p, tz, pz = slots(number)
            live = jnp.where(number < last, 1.0, 0.0)
            tower[pl.ds(u, 4, stride=8), :] = towers[
                pl.ds(tz * 256 + (t & 63), 4, stride=64), :
            ] * jnp.where(row == 3, live, 1.0)
            plate[pl.ds(u, 4, stride=8), :] = plates[
                pl.ds(pz * 256 + (p & 63), 4, stride=64), :
            ]

    def add_up(group):
        for u in range(8):
            t, p, tz, pz = slots(first + group * 8 + u)
            t, p = tz * 192 + (t & 63), pz * 192 + (p & 63)
            tower_total[pl.ds(t, 3, stride=64), :] += tower_out[pl.ds(u, 3, stride=8), :]
            plate_total[pl.ds(p, 3, stride=64), :] -= plate_out[pl.ds(u, 3, stride=8), :]

    def step(group, _):
        tower_planes = [tower[8 * c : 8 * c + 8, :] for c in range(4)]
        plate_planes = [plate[8 * c : 8 * c + 8, :] for c in range(4)]
        fetch(group + 1)
        add_up(group - 1)
        tower_force, plate_force = eight_pairs(tower_planes, plate_planes, spun, pulled)
        for c in range(3):
            tower_out[8 * c : 8 * c + 8, :] = tower_force[c]
            plate_out[8 * c : 8 * c + 8, :] = plate_force[c]
        return 0

    @pl.when(groups > 0)
    def _():
        tower_out[...] = jnp.zeros_like(tower_out)
        plate_out[...] = jnp.zeros_like(plate_out)
        fetch(0)
        lax.fori_loop(0, groups, step, 0)
        add_up(groups - 1)


def sweep_scratch():
    return [
        pltpu.VMEM((32, 128), f32),
        pltpu.VMEM((32, 128), f32),
        pltpu.VMEM((4 * LOW, 8, 128), f32),
        pltpu.VMEM((3 * LOW, 8, 128), f32),
        pltpu.VMEM((24, 128), f32),
        pltpu.VMEM((24, 128), f32),
    ]


def fill(target, block, source, lifts, strength):
    for c in range(4):
        start = block * 256 + c * 64
        values = source[c * 64 : c * 64 + 64, :]
        if c < 3:
            values = values * SCALE if isinstance(lifts[c], int) else (values + lifts[c]) * SCALE
        elif strength:
            values = values * STRENGTH
        target[start : start + 64, :] = values


def edge_of(clusters):
    return 2.4 * (clusters / 8.0) ** (1.0 / 3.0)


def sort_pairs(pairs, live, side, listing, order):
    for block in range(9):
        dx, dy = block // 3 - 1, block % 3 - 1
        if dx == 0:
            place = 1 - dy * side[1]
        else:
            place = jnp.where(side[0] == dx, 0, 3)
            if dy:
                place = place + jnp.where(side[1] == dy, 1, 2)
        order[block] = place * 64

    def step(chunk, taken):
        for u in range(8):
            number = chunk * 8 + u
            t, p = pairs[0, number], pairs[1, number]
            block = p >> 6
            across = jnp.logical_or(p < 192, p >= 384)
            home = jnp.logical_and((t >> 6) == 1, block == 4)
            entry = jnp.where(home, t & 63, jnp.where(side[2] > 0, t, (t & 63) + 128 - (t & 192))) << 10
            entry = entry | (jnp.where(home, 0, order[block]) + (p & 63))
            shift = jnp.where(home, 0, jnp.where(across, 20, 10))
            place = (shift << 5) + ((taken >> shift) & 1023)
            dead = number >= live
            listing[jnp.where(dead, 3 * SLOTS + 7, place)] = entry
            taken = taken + jnp.where(dead, 0, jnp.int32(1) << shift)
        return taken

    taken = lax.fori_loop(0, (live + 7) // 8, step, jnp.int32(0))
    for kind in range(3):
        listing[3 * SLOTS + kind] = (taken >> (10 * kind)) & 1023
    for axis in range(3):
        listing[3 * SLOTS + 3 + axis] = side[axis]


def edges(listing, atoms):
    edge = edge_of(atoms.shape[0] // 4)
    return [listing[3 * SLOTS + 3 + axis].astype(f32) * edge for axis in range(3)]


def own_end(listing, stage):
    own_count = listing[3 * SLOTS]
    flat_groups = (listing[3 * SLOTS + 1] + 7) // 8
    second = FIRST_OWN + jnp.maximum(SECOND_GROUPS - flat_groups, 0) * 8
    ends = [0, FIRST_OWN, second, second + THIRD_OWN, 2 * SLOTS]
    return jnp.minimum(own_count, ends[stage])


def first_kernel(
    pairs, count, side, atoms, listing, own, order, towers, plates, totals, *scratch
):
    fill(towers, 0, atoms, (0, 0, 0), True)
    fill(plates, 0, atoms, (0, 0, 0), False)
    own[...] = jnp.zeros_like(own)
    totals[...] = jnp.zeros_like(totals)
    sort_pairs(pairs, count[0], side, listing, order)
    sweep(listing, 0, 0, own_end(listing, 1), 0, towers, plates, own, totals, scratch)
    own[...] += totals[...]


def second_kernel(
    listing, atoms, inner, outer, under, over, before,
    own, to_inner, to_outer, to_under, to_over,
    towers, plates, tower_total, plate_total, *scratch,
):
    _, along, up = edges(listing, atoms)
    fill(towers, 0, under, (0, 0, -up), True)
    fill(towers, 1, atoms, (0, 0, 0), True)
    fill(towers, 2, over, (0, 0, up), True)
    fill(plates, 0, inner, (0, along, 0), False)
    fill(plates, 1, atoms, (0, 0, 0), False)
    fill(plates, 2, outer, (0, -along, 0), False)
    tower_total[...] = jnp.zeros_like(tower_total)
    plate_total[...] = jnp.zeros_like(plate_total)
    shared = (towers, plates, tower_total, plate_total, scratch)
    sweep(listing, SLOTS, 0, listing[3 * SLOTS + 1], 0, *shared)
    sweep(listing, 0, own_end(listing, 1), own_end(listing, 2), 1, *shared)
    own[...] = before[...] + tower_total[192:384, :] + plate_total[192:384, :]
    to_under[...] = tower_total[0:192, :]
    to_over[...] = tower_total[384:576, :]
    to_inner[...] = plate_total[0:192, :]
    to_outer[...] = plate_total[384:576, :]


def third_kernel(
    listing, atoms, under, over, mate, mate_inner, mate_outer, far, corner, far_outer,
    before, was_under, was_over,
    own, to_mate, to_far, to_corner, to_under, to_over,
    towers, plates, tower_total, plate_total, *scratch,
):
    across, along, up = edges(listing, atoms)
    fill(towers, 0, under, (0, 0, -up), True)
    fill(towers, 1, atoms, (0, 0, 0), True)
    fill(towers, 2, over, (0, 0, up), True)
    fill(plates, 0, mate, (across, 0, 0), False)
    fill(plates, 1, mate_inner, (across, along, 0), False)
    fill(plates, 2, mate_outer, (across, -along, 0), False)
    fill(plates, 3, far, (-across, 0, 0), False)
    fill(plates, 4, corner, (-across, along, 0), False)
    fill(plates, 5, far_outer, (-across, -along, 0), False)
    tower_total[0:192, :] = was_under[...]
    tower_total[192:384, :] = before[...]
    tower_total[384:576, :] = was_over[...]
    plate_total[...] = jnp.zeros_like(plate_total)
    across_count = listing[3 * SLOTS + 2]
    shared = (towers, plates, tower_total, plate_total, scratch)
    sweep(listing, 2 * SLOTS, 0, across_count, 0, *shared)
    own[...] = tower_total[192:384, :]
    to_under[...] = tower_total[0:192, :]
    to_over[...] = tower_total[384:576, :]
    to_mate[...] = plate_total[0:576, :]
    to_far[0:192, :] = plate_total[576:768, :]
    to_far[192:384, :] = plate_total[960:1152, :]
    to_corner[...] = plate_total[768:960, :]


def own_kernel(stage, listing, atoms, before, own, towers, plates, totals, *scratch):
    fill(towers, 0, atoms, (0, 0, 0), True)
    fill(plates, 0, atoms, (0, 0, 0), False)
    own[...] = before[...]
    totals[...] = jnp.zeros_like(totals)
    shared = (towers, plates, own, totals, scratch)
    sweep(listing, 0, own_end(listing, stage - 1), own_end(listing, stage), 0, *shared)
    own[...] += totals[...]


def bond_kernel(atoms, velocities, inverse_mass, bond_partner, *refs):
    parts, (forces, moved) = refs[:-2], refs[-2:]
    rows = inverse_mass.shape[0]
    lane = lax.broadcasted_iota(jnp.int32, (rows, 128), 1)
    heads = lane - lane % 4
    corners = [heads + k for k in range(4)]

    def taken(values, index):
        return jnp.take_along_axis(values, index, axis=1)

    partner = bond_partner[...]
    mass = inverse_mass[...]
    hydro = partner != lane
    hits = [taken(partner, corner) == lane for corner in corners]
    bond, shift = [], []
    for c in range(3):
        place = slice(c * rows, c * rows + rows)
        force = parts[0][place, :]
        for part in parts[1:]:
            force = force + part[place, :]
        forces[place, :] = force
        kicked = velocities[place, :] + TIME_STEP * FORCE_UNIT * mass * force
        shift.append(TIME_STEP * kicked)
        coords = atoms[place, :]
        bond.append(coords - taken(coords, partner))
    square = bond[0] * bond[0] + bond[1] * bond[1] + bond[2] * bond[2]
    paired = mass + taken(mass, partner)
    for _ in range(ITERS):
        gap = [bond[c] + (shift[c] - taken(shift[c], partner)) for c in range(3)]
        excess = gap[0] * gap[0] + gap[1] * gap[1] + gap[2] * gap[2] - square
        along = gap[0] * bond[0] + gap[1] * bond[1] + gap[2] * bond[2]
        slope = 2.0 * along * paired
        factor = jnp.where(hydro, excess / jnp.where(hydro, slope, 1.0), 0.0)
        for c in range(3):
            delta = factor * bond[c]
            back = None
            for corner, hit in zip(corners, hits):
                back = plus(back, jnp.where(hit, taken(delta, corner), 0.0))
            shift[c] = shift[c] + mass * (back - delta)
    for c in range(3):
        moved[c * rows : c * rows + rows, :] = shift[c] / TIME_STEP


def planes(count=1):
    return jax.ShapeDtypeStruct((count * 192, 128), f32)


def run(kernel, outs, scalars, arrays, scratch, microseconds):
    smem = pl.BlockSpec(memory_space=pltpu.SMEM)
    vmem = pl.BlockSpec(memory_space=pltpu.VMEM)
    return pl.pallas_call(
        kernel,
        out_shape=outs,
        in_specs=[smem] * len(scalars) + [vmem] * len(arrays),
        out_specs=[smem if out.dtype == jnp.int32 else vmem for out in outs],
        scratch_shapes=scratch,
        compiler_params=pltpu.CompilerParams(vmem_limit_bytes=32 * 1024 * 1024),
        cost_estimate=pl.CostEstimate(
            flops=int(microseconds * 4e6), bytes_accessed=int(microseconds * 3e6), transcendentals=0
        ),
    )(*scalars, *arrays)


def local(atoms, velocities, inverse_mass, bond_partner, cluster_pairs, pair_count):
    own = atoms.reshape(256, 128)
    blocks = lambda count, rows: pltpu.VMEM((count * rows, 128), f32)
    inner = swapped(own, "gy", False)
    outer = swapped(own, "gy", True)
    under = swapped(own, "gz", True)
    over = swapped(own, "gz", False)
    far = swapped(own, "gx", True)
    corner = swapped_corner(own)
    mate = swapped(own, "gx", False)
    side = jnp.stack([1 - 2 * (lax.axis_index(axis) % 2) for axis in ("gx", "gy", "gz")])
    listing, part = run(
        first_kernel,
        [jax.ShapeDtypeStruct((3 * SLOTS + 8,), jnp.int32), planes()],
        [cluster_pairs.reshape(2, -1), pair_count.reshape(1), side.astype(jnp.int32)],
        [own],
        [pltpu.SMEM((16,), jnp.int32)]
        + [blocks(1, 256), blocks(1, 256), blocks(1, 192)]
        + sweep_scratch(),
        4,
    )
    over, under, inner, outer, far, corner, mate, part = lax.optimization_barrier(
        (over, under, inner, outer, far, corner, mate, part)
    )
    far_outer = swapped(outer, "gx", True)
    mate_inner = swapped(inner, "gx", False)
    mate_outer = swapped(outer, "gx", False)
    part, to_inner, to_outer, to_under, to_over = run(
        second_kernel,
        [planes()] * 5,
        [listing],
        [own, inner, outer, under, over, part],
        [blocks(3, 256), blocks(3, 256), blocks(3, 192), blocks(3, 192)] + sweep_scratch(),
        6,
    )
    part, to_mate, to_far, to_corner, to_under, to_over = run(
        third_kernel,
        [planes(), planes(3), planes(2), planes(), planes(), planes()],
        [listing],
        [own, under, over, mate, mate_inner, mate_outer, far, corner, far_outer]
        + [part, to_under, to_over],
        [blocks(3, 256), blocks(6, 256), blocks(3, 192), blocks(6, 192)] + sweep_scratch(),
        4,
    )
    from_mate = swapped(to_mate, "gx", False)
    from_far = swapped(to_far, "gx", True)
    from_corner = swapped_corner(to_corner)
    from_under = swapped(to_under, "gz", True)
    from_over = swapped(to_over, "gz", False)
    own_scratch = [blocks(1, 256), blocks(1, 256), blocks(1, 192)] + sweep_scratch()
    (part,) = run(
        functools.partial(own_kernel, 3), [planes()], [listing], [own, part], own_scratch, 5
    )
    to_inner = to_inner + from_mate[192:384]
    to_outer = to_outer + from_mate[384:576] + from_far[192:384]
    to_inner, to_outer, part = lax.optimization_barrier((to_inner, to_outer, part))
    from_inner = swapped(to_inner, "gy", False)
    from_outer = swapped(to_outer, "gy", True)
    (part,) = run(
        functools.partial(own_kernel, 4), [planes()], [listing], [own, part], own_scratch, 4
    )
    forces, moved = run(
        bond_kernel,
        [planes(), planes()],
        [],
        [
            own,
            velocities.reshape(192, 128),
            inverse_mass.reshape(64, 128),
            bond_partner.reshape(64, 128),
            part,
            from_mate,
            from_far,
            from_corner,
            from_over,
            from_under,
            from_inner,
            from_outer,
        ],
        [],
        2,
    )
    return (forces.reshape(3, 1, 1, 64, 128), moved.reshape(3, 1, 1, 64, 128))


def solution(mesh):
    return jax.shard_map(
        local,
        mesh=mesh,
        in_specs=(
            P(None, "gx", "gy", "gz", None),
            P(None, "gx", "gy", "gz", None),
            P("gx", "gy", "gz", None),
            P("gx", "gy", "gz", None),
            P(None, "gx", "gy", "gz"),
            P("gx", "gy", "gz"),
        ),
        out_specs=(P(None, "gx", "gy", "gz", None), P(None, "gx", "gy", "gz", None)),
        check_vma=False,
    )
```
